32 devices in a mesh: grp: 2 (over y), wk: 8 (over z, x), ar: 2 (over core).
Axes of the slice: x: 2, y: 2, z: 4, core: 2. Of those that a mesh axis runs over, the one named last changes fastest.
Arguments:
- latent: float32 [48, 16, 2048], P('grp', 'wk', 'ar'), parts along dimension 0, may hold values from -3 to 3
- log_offset: float32 [48, 16, 2048], P('grp', 'wk', 'ar'), parts along dimension 0, may hold values from -1 to 1.5
- case_counts: int32 [48, 16, 2048], P('grp', 'wk', 'ar'), parts along dimension 0, may hold values from 0 to 9
- tau: float32 [24], replicated, may hold values from 0.3 to 3
- phi_one: float32 [24], replicated, may hold values from 0.2 to 1.2
- phi_two: float32 [24], replicated, may hold values from -0.5 to 0.3
- blocks: float32 [16, 4, 128, 128], P('ar'), as said below
- block_index: int32 [16, 4], P('ar'), may hold values from 0 to 15, as said below
- block_count: int32 [16], P('ar'), may hold values from 2 to 4, as said below
Outputs:
- updated: float32 [48, 16, 2048], P('grp', 'wk', 'ar'), parts along dimension 0
The draws below stay inside these ranges and needn't reach their ends.
There are 2 independent parts, one for each index of `grp`. The reference program is written for one: setup_inputs(seed, part) draws one part's arguments, and reference() takes and returns one part's arrays. A program takes and returns all parts, laid end to end along the dimension named above; an argument that names none is the same for every part. Nothing has to cross between parts.
Inputs may be any that keep to these rules, and one draw needn't show every extreme that they name: `block_index`: slot 0 of block row b lists b; slots below block_count list distinct blocks within two of b, those of b - 1 and b + 1 that exist always among them; unused slots list b. The pattern is symmetric: row b lists c where row c lists b. `block_count`: some block row uses all 4 slots and some uses 2. `blocks`: the block that row b lists for c is the transpose of the block that row c lists for b; the assembled spatial matrix has entries off the diagonal in [-1 / 512, 1 / 512] and a diagonal larger than the sum of magnitudes of the rest of its row.
All inputs are finite; a program needn't handle non-finite values.
Results may differ from the reference program's by a relative error of at most 0.00023.
Values sent between devices are 32-bit elements; how exact they have to be, the bound alone decides.
A program may use at most 64 MiB of HBM per device.

```python
import math
import jax
import jax.numpy as jnp
from jax import lax

CANCERS = 24
BLK = 128
SLOTS = 4
ITERS = 3
WEEKS = 16
AREA_BLOCKS = 16
AREAS = 2048


def pattern(key):
    rows = jnp.arange(AREA_BLOCKS)
    bits = jax.random.randint(key, (AREA_BLOCKS,), 0, 2)
    bits = jnp.where(rows == 1, 1, jnp.where(rows == 0, 0, bits))
    allowed = (rows % 4 <= 1) & (rows + 2 < AREA_BLOCKS)
    upward = allowed & (bits == 1)
    downward = jnp.where(rows >= 2, upward[jnp.clip(rows - 2, 0, AREA_BLOCKS - 1)], False)
    offsets = jnp.array([0, -2, -1, 1, 2], dtype=jnp.int32)
    columns = rows[:, None] + offsets[None, :]
    inside = (columns >= 0) & (columns < AREA_BLOCKS)
    always = jnp.ones((AREA_BLOCKS,), dtype=bool)
    present = jnp.stack([always, downward, always, always, upward], axis=1)
    valid = inside & present
    position = jnp.arange(5, dtype=jnp.int32)[None, :]
    scores = jnp.where(valid, position, position + 5)
    order = jnp.argsort(scores, axis=1, stable=True)[:, :SLOTS]
    chosen = jnp.take_along_axis(columns, order, axis=1)
    counted = jnp.sum(valid.astype(jnp.int32), axis=1).astype(jnp.int32)
    slot = jnp.arange(SLOTS)[None, :]
    index = jnp.where(slot < counted[:, None], chosen, rows[:, None]).astype(jnp.int32)
    return (index, counted)


def draw_block_index(key, part):
    index, counted = pattern(key)
    return index


def draw_block_count(key, part):
    index, counted = pattern(key)
    return counted


def draw_blocks(key, part):
    index, counted = pattern(key)
    own_key = jax.random.fold_in(key, 7)
    diag_key = jax.random.fold_in(key, 11)
    negative = jax.random.bernoulli(own_key, 0.6, (AREA_BLOCKS, AREA_BLOCKS, BLK, BLK))
    table = jnp.where(negative, -1.0, 1.0).astype(jnp.float32)
    rows = jnp.arange(AREA_BLOCKS)
    inner = jnp.arange(BLK)
    global_row = rows[:, None, None, None] * BLK + inner[None, None, :, None]
    global_col = rows[None, :, None, None] * BLK + inner[None, None, None, :]
    upper = global_row < global_col
    paired = jnp.where(upper, table, jnp.transpose(table, (1, 0, 3, 2)))
    chosen = paired[rows[:, None], index]
    eye = jnp.eye(BLK, dtype=jnp.float32)
    weight = 1.0 / (BLK * SLOTS)
    off_part = weight * chosen * (1.0 - eye)[None, None, :, :]
    diag_values = jax.random.uniform(diag_key, (AREA_BLOCKS, BLK), jnp.float32, 1.01, 1.3)
    own_slot = (jnp.arange(SLOTS) == 0).astype(jnp.float32)
    diag_part = own_slot[None, :, None, None] * diag_values[:, None, :, None] * eye[None, None, :, :]
    return (off_part + diag_part).astype(jnp.float32)


def place_ends(values, key, low, high):
    index_at = [jax.random.randint(jax.random.fold_in(key, axis), (), 0, length) for axis, length in enumerate(values.shape)]
    longest = values.shape.index(max(values.shape))
    neighbour = index_at[:longest] + [(index_at[longest] + 1) % values.shape[longest]] + index_at[longest + 1:]
    return values.at[tuple(index_at)].set(low).at[tuple(neighbour)].set(high)


def block_levels(rng, shape, cuts, smallest, top_value):
    def one(dim, blocks):
        steps = jax.random.uniform(jax.random.fold_in(jax.random.fold_in(rng, 6), dim), (blocks,), jnp.float32, smallest / len(cuts), top_value / len(cuts))
        return jnp.repeat(jnp.exp(steps), shape[dim] // blocks).reshape((-1,) + (1,) * (len(shape) - dim - 1))

    factor_of = one(*cuts[0])
    for cut in cuts[1:]:
        factor_of = factor_of * one(*cut)
    return factor_of


def centred(stream_key, dims, scale, limit, shards=(), held_as=jnp.bfloat16):
    values = jax.random.normal(stream_key, dims, jnp.float32) * scale
    if len(shards) > 0:
        values = block_levels(stream_key, dims, shards, -0.22, 0.18) * values
    return jnp.clip(values, min=-limit, max=limit).astype(held_as)


def setup_inputs(seed: int = 0, part: int = 0) -> dict:
    streams_of = jax.random.split(jax.random.key(seed), 10)
    part_keys = jax.random.split(jax.random.fold_in(streams_of[9], part), 10)
    return {
        "latent": centred(part_keys[0], (CANCERS, WEEKS, AREAS), 0.5, 3.0, ((1, 8), (2, 2)), jnp.float32),
        "log_offset": jnp.clip(-1.0 + 2.5 * jax.random.uniform(part_keys[1], (CANCERS, WEEKS, AREAS), jnp.float32) ** block_levels(part_keys[1], (CANCERS, WEEKS, AREAS), ((1, 8), (2, 2)), -0.2, 0.2), -1.0, 1.5),
        "case_counts": place_ends(jax.random.randint(part_keys[2], (CANCERS, WEEKS, AREAS), 0, 10), jax.random.fold_in(part_keys[2], 1), 0, 9).astype(jnp.int32),
        "tau": jnp.clip(jnp.exp(jax.random.uniform(streams_of[3], (CANCERS,), jnp.float32, math.log(0.3), math.log(3.0))), 0.3, 3.0),
        "phi_one": jnp.clip(jax.random.uniform(streams_of[4], (CANCERS,), jnp.float32, 0.2, 1.2), 0.2, 1.2),
        "phi_two": jnp.clip(jax.random.uniform(streams_of[5], (CANCERS,), jnp.float32, -0.5, 0.3), -0.5, 0.3),
        "blocks": draw_blocks(jax.random.fold_in(streams_of[9], 71), part),
        "block_index": draw_block_index(jax.random.fold_in(streams_of[9], 71), part),
        "block_count": draw_block_count(jax.random.fold_in(streams_of[9], 71), part),
    }


def temporal(field, first_lag, second_lag):
    lower = jnp.pad(field, ((0, 0), (2, 0), (0, 0)))
    innovation = lower[:, 2:] - first_lag * lower[:, 1:-1] - second_lag * lower[:, :-2]
    upper = jnp.pad(innovation, ((0, 0), (0, 2), (0, 0)))
    return upper[:, :-2] - first_lag * upper[:, 1:-1] - second_lag * upper[:, 2:]


def spatial(field, masked, block_index):
    weeks_all = field.shape[1]
    areas_all = field.shape[2]
    block_rows = areas_all // BLK

    def per_cancer(plane):
        blocks_of = plane.reshape(weeks_all, block_rows, BLK)[:, block_index, :]
        result = jnp.einsum("wnsi,nsij->wnj", blocks_of, masked, precision=lax.Precision.HIGHEST)
        return result.reshape(weeks_all, areas_all)

    return lax.map(per_cancer, field)


def reference(latent, log_offset, case_counts, tau, phi_one, phi_two, blocks, block_index, block_count):
    slot_live = (jnp.arange(SLOTS)[None, :] < block_count[:, None]).astype(jnp.float32)
    masked = blocks * slot_live[:, :, None, None]
    first_lag = phi_one[:, None, None]
    second_lag = phi_two[:, None, None]
    prior_scale = tau[:, None, None]

    def prior(field):
        return prior_scale * spatial(temporal(field, first_lag, second_lag), masked, block_index)

    mean = jnp.exp(log_offset + latent)

    def operate(field):
        return prior(field) + mean * field

    gradient = case_counts.astype(jnp.float32) - mean - prior(latent)
    search = jnp.zeros_like(latent)
    residual = gradient
    direction = gradient
    norm_now = jnp.sum(residual * residual, axis=(1, 2))[:, None, None]
    for iteration in range(ITERS):
        image = operate(direction)
        alpha = norm_now / jnp.sum(direction * image, axis=(1, 2))[:, None, None]
        search = search + alpha * direction
        residual = residual - alpha * image
        norm_next = jnp.sum(residual * residual, axis=(1, 2))[:, None, None]
        direction = residual + (norm_next / norm_now) * direction
        norm_now = norm_next
    return latent + search
```

```python
import functools

import jax
import jax.numpy as jnp
from jax import lax
from jax.experimental import pallas as pl
from jax.experimental.pallas import tpu as pltpu
from jax.sharding import PartitionSpec as P

ITERS = 3
MESH = pl.DeviceIdType.MESH


def extended(value, sides, width):
    for axis, dim in sides:
        peers, length = (lax.axis_size(axis), value.shape[dim])
        up = [(i, (i + 1) % peers) for i in range(peers - 1)]
        down = [(j, i) for i, j in up]
        last = lax.slice_in_dim(value, length - width, length, axis=dim)
        initial = lax.slice_in_dim(value, 0, width, axis=dim)
        before = lax.ppermute(last, axis, up)
        after = lax.ppermute(initial, axis, down)
        value = jnp.concatenate([before, value, after], axis=dim)
    return value


def temporal(field, first_lag, second_lag):
    weeks_here = field.shape[1]
    weeks_total = lax.axis_size("wk") * weeks_here
    padded = extended(field, (("wk", 1),), 2)
    innovation = (
        padded[:, 2 : weeks_here + 4]
        - first_lag * padded[:, 1 : weeks_here + 3]
        - second_lag * padded[:, 0 : weeks_here + 2]
    )
    week_number = lax.axis_index("wk") * weeks_here + jnp.arange(weeks_here + 2)
    innovation = jnp.where((week_number < weeks_total)[None, :, None], innovation, 0.0)
    return (
        innovation[:, 0:weeks_here]
        - first_lag * innovation[:, 1 : weeks_here + 1]
        - second_lag * innovation[:, 2 : weeks_here + 2]
    )


def spatial(field, masked, block_index):
    cancers, weeks_here, areas_here = field.shape
    rows_here, slot_total, width, unused = masked.shape
    padded = extended(field, (("ar", 2),), 2 * width)
    first_row = lax.axis_index("ar") * rows_here - 2
    local_index = block_index - first_row
    blocks_of = padded.reshape(cancers, weeks_here, rows_here + 4, width)[:, :, local_index, :]
    result = jnp.einsum("cwnsi,nsij->cwnj", blocks_of, masked, precision=lax.Precision.HIGHEST)
    return result.reshape(cancers, weeks_here, areas_here)


def global_sum(values):
    return lax.psum(values, ("wk", "ar"))[:, None, None]


def local(latent, log_offset, case_counts, tau, phi_one, phi_two, blocks, block_index, block_count):
    slot_live = (jnp.arange(blocks.shape[1])[None, :] < block_count[:, None]).astype(jnp.float32)
    masked = blocks * slot_live[:, :, None, None]
    first_lag = phi_one[:, None, None]
    second_lag = phi_two[:, None, None]
    prior_scale = tau[:, None, None]

    def prior(field):
        return prior_scale * spatial(temporal(field, first_lag, second_lag), masked, block_index)

    mean = jnp.exp(log_offset + latent)
    gradient = case_counts.astype(jnp.float32) - mean - prior(latent)
    search = jnp.zeros_like(latent)
    residual = gradient
    direction = gradient
    norm_now = global_sum(jnp.sum(residual * residual, axis=(1, 2)))
    for iteration in range(ITERS):
        image = prior(direction) + mean * direction
        curve = lax.psum(jnp.sum(direction * image, axis=(1, 2)), ("wk", "ar"))[:, None, None]
        alpha = norm_now / curve
        search = search + alpha * direction
        residual = residual - alpha * image
        norm_next = global_sum(jnp.sum(residual * residual, axis=(1, 2)))
        direction = residual + norm_next / norm_now * direction
        norm_now = norm_next
    return latent + search


def site_kernel(
    peers, areas, per_chip, weeks_here, rows_here, slot_total,
    latent, log_offset, case_counts, tau, phi_one, phi_two, blocks, slot_index, slot_count,
    out,
    packed, field, matrix, wide, index_all, count_all,
    temporal_rows, operand, product, mean, direction, residual, search, outgoing, returned,
    send_sem, recv_sem, matrix_sem, table_sem, back_sem, return_sem,
):
    me = lax.axis_index("wk")
    half = lax.axis_index("ar")
    width = blocks.shape[-1]
    site_slots = -(-per_chip // areas)
    weeks = peers * weeks_here
    rows = areas * rows_here
    sites_here = jnp.minimum(site_slots, per_chip - half * site_slots)

    barrier = pltpu.get_barrier_semaphore()
    for step in range(1, peers * areas):
        other = lax.rem(me * areas + half + step, peers * areas)
        pl.semaphore_signal(
            barrier, inc=1, device_id={"wk": other // areas, "ar": lax.rem(other, areas)}, device_id_type=MESH
        )

    own_rows = pl.ds(half * rows_here, rows_here)
    own_matrix = pltpu.make_async_copy(blocks, matrix.at[own_rows], matrix_sem.at[0])
    own_matrix.start()
    own_index = pltpu.make_async_copy(slot_index, index_all.at[half], table_sem.at[0])
    own_index.start()
    own_count = pltpu.make_async_copy(slot_count, count_all.at[half], table_sem.at[1])
    own_count.start()

    for site in range(peers * per_chip):
        for week in range(weeks_here):
            row = pl.ds(site * rows_here * weeks_here + week, rows_here, stride=weeks_here)
            now = latent[row, :]
            rate = jnp.exp(log_offset[row, :] + now)
            packed[site, 0, week] = now
            packed[site, 1, week] = rate
            packed[site, 2, week] = case_counts[row, :].astype(jnp.float32) - rate

    pl.semaphore_wait(barrier, peers * areas - 1)

    twin = {"ar": 1 - half}
    twin_rows = pl.ds((1 - half) * rows_here, rows_here)
    to_twin = [
        pltpu.make_async_remote_copy(
            slot_index, index_all.at[half], table_sem.at[2], table_sem.at[3], device_id=twin, device_id_type=MESH
        ),
        pltpu.make_async_remote_copy(
            slot_count, count_all.at[half], table_sem.at[4], table_sem.at[5], device_id=twin, device_id_type=MESH
        ),
        pltpu.make_async_remote_copy(
            blocks, matrix.at[own_rows], matrix_sem.at[1], matrix_sem.at[2], device_id=twin, device_id_type=MESH
        ),
    ]
    for copy in to_twin:
        copy.start()

    def scatter(j, step, starting):
        core, slot = j // site_slots, j % site_slots
        peer = lax.rem(me + step, peers)
        site = peer * per_chip + j
        source, target = packed.at[site], field.at[slot, me, half]
        arrived = recv_sem.at[slot, me, half]

        def away():
            copy = pltpu.make_async_remote_copy(
                source, target, send_sem.at[j, step], arrived,
                device_id={"wk": peer, "ar": core}, device_id_type=MESH,
            )
            copy.start() if starting else copy.wait_send()

        def here():
            pltpu.make_async_copy(source, target, arrived).start()

        if step == 0:
            pl.when(half != core)(away)
            if starting:
                pl.when(half == core)(here)
        else:
            away()

    for j in range(per_chip):
        for step in range(peers):
            scatter(j, step, True)

    def spread(block_row):
        for slot in range(slot_total):
            live = slot < count_all[block_row // rows_here, lax.rem(block_row, rows_here)]
            block = jnp.where(live, matrix[block_row, slot], 0.0)
            high = block.astype(jnp.bfloat16)
            low = (block - high.astype(jnp.float32)).astype(jnp.bfloat16)
            wide[block_row, slot * width : (slot + 1) * width, 0:width] = high
            wide[block_row, slot * width : (slot + 1) * width, width : 2 * width] = low

    own_matrix.wait()
    own_index.wait()
    own_count.wait()

    @pl.loop(0, rows_here)
    def _(n):
        spread(half * rows_here + n)

    for copy in to_twin:
        copy.wait_recv()

    @pl.loop(0, rows_here)
    def _(n):
        spread((1 - half) * rows_here + n)

    def prior(first_lag, second_lag):
        for a in range(areas):
            part = [direction[pl.ds(t * rows + a * rows_here, rows_here), :] for t in range(weeks)]
            inner = []
            for t in range(weeks):
                value = part[t]
                if t >= 1:
                    value = value - first_lag * part[t - 1]
                if t >= 2:
                    value = value - second_lag * part[t - 2]
                inner.append(value)
            for t in range(weeks):
                value = inner[t]
                if t + 1 < weeks:
                    value = value - first_lag * inner[t + 1]
                if t + 2 < weeks:
                    value = value - second_lag * inner[t + 2]
                temporal_rows[pl.ds(t * rows + a * rows_here, rows_here), :] = value
        for g in range(rows):
            value = temporal_rows[pl.ds(g, weeks, stride=rows), :]
            high = value.astype(jnp.bfloat16)
            operand[g, 0:weeks] = high
            operand[g, weeks : 2 * weeks] = (value - high.astype(jnp.float32)).astype(jnp.bfloat16)
        for n in range(rows):
            a, b = n // rows_here, n % rows_here
            left = jnp.concatenate([operand[index_all[a, s, b]] for s in range(slot_total)], axis=1)
            both = jnp.dot(left, wide[n], preferred_element_type=jnp.float32)
            value = both[0:weeks, 0:width] + (both[0:weeks, width:] + both[weeks:, 0:width])
            product[pl.ds(n, weeks, stride=rows), :] = value

    def total(values):
        return jnp.sum(values, axis=(0, 1), keepdims=True)

    def give(slot, step, a, starting):
        peer = lax.rem(me + step, peers)
        source = outgoing.at[slot, peer, a]
        site = me * per_chip + half * site_slots + slot
        target, arrived = returned.at[site], return_sem.at[site]

        def away():
            copy = pltpu.make_async_remote_copy(
                source, target, back_sem.at[slot, step, a], arrived,
                device_id={"wk": peer, "ar": a}, device_id_type=MESH,
            )
            copy.start() if starting else copy.wait_send()

        def here():
            pltpu.make_async_copy(source, target, arrived).start()

        if step == 0:
            pl.when(half != a)(away)
            if starting:
                pl.when(half == a)(here)
        else:
            away()

    @pl.loop(0, sites_here)
    def _(slot):
        site = me * per_chip + half * site_slots + slot
        scale, first_lag, second_lag = tau[site], phi_one[site], phi_two[site]
        for w in range(peers):
            for a in range(areas):
                pltpu.make_async_copy(packed.at[0], field.at[slot, w, a], recv_sem.at[slot, w, a]).wait()
        for w in range(peers):
            for a in range(areas):
                for t in range(weeks_here):
                    row = pl.ds((w * weeks_here + t) * rows + a * rows_here, rows_here)
                    direction[row, :] = field[slot, w, a, 0, t]
                    mean[row, :] = field[slot, w, a, 1, t]
                    residual[row, :] = field[slot, w, a, 2, t]
        prior(first_lag, second_lag)
        gradient = residual[...] - scale * product[...]
        residual[...] = gradient
        direction[...] = gradient
        search[...] = jnp.zeros_like(gradient)

        def iteration(_, norm_now):
            prior(first_lag, second_lag)
            image = scale * product[...] + mean[...] * direction[...]
            alpha = norm_now / total(direction[...] * image)
            search[...] += alpha * direction[...]
            after = residual[...] - alpha * image
            residual[...] = after
            norm_next = total(after * after)
            direction[...] = after + (norm_next / norm_now) * direction[...]
            return norm_next

        lax.fori_loop(0, ITERS, iteration, total(gradient * gradient))
        for w in range(peers):
            for a in range(areas):
                for t in range(weeks_here):
                    row = pl.ds((w * weeks_here + t) * rows + a * rows_here, rows_here)
                    outgoing[slot, w, a, t] = search[row, :]
        for step in range(peers):
            for a in range(areas):
                give(slot, step, a, True)

    for j in range(per_chip):
        for w in range(peers):
            site = w * per_chip + j
            pltpu.make_async_copy(outgoing.at[0, 0, 0], returned.at[site], return_sem.at[site]).wait()
            for week in range(weeks_here):
                row = pl.ds(site * rows_here * weeks_here + week, rows_here, stride=weeks_here)
                out[row, :] = latent[row, :] + returned[site, week]

    for copy in to_twin:
        copy.wait_send()
    for j in range(per_chip):
        for step in range(peers):
            scatter(j, step, False)

    @pl.loop(0, sites_here)
    def _(slot):
        for step in range(peers):
            for a in range(areas):
                give(slot, step, a, False)


def by_site(
    peers, areas, latent, log_offset, case_counts, tau, phi_one, phi_two, blocks, block_index, block_count
):
    cancers, weeks_here, areas_here = latent.shape
    rows_here, slot_total, width, _ = blocks.shape
    if cancers % peers or areas != 2 or rows_here % 8 or (peers * weeks_here) % 16:
        return local(latent, log_offset, case_counts, tau, phi_one, phi_two, blocks, block_index, block_count)
    per_chip = cancers // peers
    site_slots = -(-per_chip // areas)
    weeks, rows = peers * weeks_here, areas * rows_here

    def as_rows(value):
        split = value.reshape(cancers, weeks_here, rows_here, width)
        return split.transpose(0, 2, 1, 3).reshape(cancers * rows_here * weeks_here, width)

    f32, bf16 = jnp.float32, jnp.bfloat16
    tile = (weeks_here, rows_here, width)
    plane = pltpu.VMEM((weeks * rows, width), f32)
    dma = pltpu.SemaphoreType.DMA
    vmem, smem = pl.BlockSpec(memory_space=pltpu.VMEM), pl.BlockSpec(memory_space=pltpu.SMEM)
    result = pl.pallas_call(
        functools.partial(site_kernel, peers, areas, per_chip, weeks_here, rows_here, slot_total),
        out_shape=jax.ShapeDtypeStruct((cancers * rows_here * weeks_here, width), f32),
        in_specs=[vmem] * 3 + [smem] * 3 + [pl.BlockSpec(memory_space=pl.ANY)] + [smem] * 2,
        out_specs=vmem,
        scratch_shapes=[
            pltpu.VMEM((cancers, 3) + tile, f32),
            pltpu.VMEM((site_slots, peers, areas, 3) + tile, f32),
            pltpu.VMEM((rows, slot_total, width, width), f32),
            pltpu.VMEM((rows, slot_total * width, 2 * width), bf16),
            pltpu.SMEM((areas, slot_total, rows_here), jnp.int32),
            pltpu.SMEM((areas, rows_here), jnp.int32),
            plane,
            pltpu.VMEM((rows, 2 * weeks, width), bf16),
            plane, plane, plane, plane, plane,
            pltpu.VMEM((site_slots, peers, areas) + tile, f32),
            pltpu.VMEM((cancers,) + tile, f32),
            dma((per_chip, peers)),
            dma((site_slots, peers, areas)),
            dma((3,)),
            dma((6,)),
            dma((site_slots, peers, areas)),
            dma((cancers,)),
        ],
        compiler_params=pltpu.CompilerParams(
            collective_id=0, has_side_effects=True, vmem_limit_bytes=40 * 1024 * 1024
        ),
    )(
        as_rows(latent), as_rows(log_offset), as_rows(case_counts), tau, phi_one, phi_two,
        blocks, block_index.T, block_count,
    )
    split = result.reshape(cancers, rows_here, weeks_here, width).transpose(0, 2, 1, 3)
    return split.reshape(latent.shape)


def solution(mesh):
    return jax.shard_map(
        functools.partial(by_site, mesh.shape["wk"], mesh.shape["ar"]),
        mesh=mesh,
        in_specs=(
            P("grp", "wk", "ar"),
            P("grp", "wk", "ar"),
            P("grp", "wk", "ar"),
            P(),
            P(),
            P(),
            P("ar", None, None, None),
            P("ar", None),
            P("ar"),
        ),
        out_specs=P("grp", "wk", "ar"),
        check_vma=False,
    )
```

```python
import functools

import jax
import jax.numpy as jnp
from jax import lax
from jax.experimental import pallas as pl
from jax.experimental.pallas import tpu as pltpu
from jax.sharding import PartitionSpec as P

ITERS = 3
MESH = pl.DeviceIdType.MESH


def extended(value, sides, width):
    for axis, dim in sides:
        peers, length = (lax.axis_size(axis), value.shape[dim])
        up = [(i, (i + 1) % peers) for i in range(peers - 1)]
        down = [(j, i) for i, j in up]
        last = lax.slice_in_dim(value, length - width, length, axis=dim)
        initial = lax.slice_in_dim(value, 0, width, axis=dim)
        before = lax.ppermute(last, axis, up)
        after = lax.ppermute(initial, axis, down)
        value = jnp.concatenate([before, value, after], axis=dim)
    return value


def temporal(field, first_lag, second_lag):
    weeks_here = field.shape[1]
    weeks_total = lax.axis_size("wk") * weeks_here
    padded = extended(field, (("wk", 1),), 2)
    innovation = (
        padded[:, 2 : weeks_here + 4]
        - first_lag * padded[:, 1 : weeks_here + 3]
        - second_lag * padded[:, 0 : weeks_here + 2]
    )
    week_number = lax.axis_index("wk") * weeks_here + jnp.arange(weeks_here + 2)
    innovation = jnp.where((week_number < weeks_total)[None, :, None], innovation, 0.0)
    return (
        innovation[:, 0:weeks_here]
        - first_lag * innovation[:, 1 : weeks_here + 1]
        - second_lag * innovation[:, 2 : weeks_here + 2]
    )


def spatial(field, masked, block_index):
    cancers, weeks_here, areas_here = field.shape
    rows_here, slot_total, width, unused = masked.shape
    padded = extended(field, (("ar", 2),), 2 * width)
    first_row = lax.axis_index("ar") * rows_here - 2
    local_index = block_index - first_row
    blocks_of = padded.reshape(cancers, weeks_here, rows_here + 4, width)[:, :, local_index, :]
    result = jnp.einsum("cwnsi,nsij->cwnj", blocks_of, masked, precision=lax.Precision.HIGHEST)
    return result.reshape(cancers, weeks_here, areas_here)


def global_sum(values):
    return lax.psum(values, ("wk", "ar"))[:, None, None]


def local(latent, log_offset, case_counts, tau, phi_one, phi_two, blocks, block_index, block_count):
    slot_live = (jnp.arange(blocks.shape[1])[None, :] < block_count[:, None]).astype(jnp.float32)
    masked = blocks * slot_live[:, :, None, None]
    first_lag = phi_one[:, None, None]
    second_lag = phi_two[:, None, None]
    prior_scale = tau[:, None, None]

    def prior(field):
        return prior_scale * spatial(temporal(field, first_lag, second_lag), masked, block_index)

    mean = jnp.exp(log_offset + latent)
    gradient = case_counts.astype(jnp.float32) - mean - prior(latent)
    search = jnp.zeros_like(latent)
    residual = gradient
    direction = gradient
    norm_now = global_sum(jnp.sum(residual * residual, axis=(1, 2)))
    for iteration in range(ITERS):
        image = prior(direction) + mean * direction
        curve = lax.psum(jnp.sum(direction * image, axis=(1, 2)), ("wk", "ar"))[:, None, None]
        alpha = norm_now / curve
        search = search + alpha * direction
        residual = residual - alpha * image
        norm_next = global_sum(jnp.sum(residual * residual, axis=(1, 2)))
        direction = residual + norm_next / norm_now * direction
        norm_now = norm_next
    return latent + search


def site_kernel(
    peers, areas, per_chip, weeks_here, rows_here, slot_total,
    latent_in, offset_in, counts_in, tau_in, one_in, two_in, blocks, slot_index, slot_count,
    out,
    latent, log_offset, case_counts, tau, phi_one, phi_two,
    packed, field, matrix, wide, index_all, count_all,
    temporal_rows, operand, product, mean, direction, residual, search, outgoing, returned,
    input_sem, send_sem, recv_sem, matrix_sem, table_sem, back_sem, return_sem,
):
    me = lax.axis_index("wk")
    half = lax.axis_index("ar")
    width = blocks.shape[-1]
    site_slots = -(-per_chip // areas)
    weeks = peers * weeks_here
    rows = areas * rows_here
    sites_here = jnp.minimum(site_slots, per_chip - half * site_slots)

    barrier = pltpu.get_barrier_semaphore()
    for step in range(1, peers * areas):
        other = lax.rem(me * areas + half + step, peers * areas)
        pl.semaphore_signal(
            barrier, inc=1, device_id={"wk": other // areas, "ar": lax.rem(other, areas)}, device_id_type=MESH
        )

    inputs = [
        pltpu.make_async_copy(source, target, input_sem.at[n])
        for n, (source, target) in enumerate(
            (
                (latent_in, latent), (offset_in, log_offset), (counts_in, case_counts),
                (tau_in, tau), (one_in, phi_one), (two_in, phi_two),
            )
        )
    ]
    for copy in inputs:
        copy.start()
    own_rows = pl.ds(half * rows_here, rows_here)
    own_matrix = pltpu.make_async_copy(blocks, matrix.at[own_rows], matrix_sem.at[0])
    own_index = pltpu.make_async_copy(slot_index, index_all.at[half], table_sem.at[0])
    own_count = pltpu.make_async_copy(slot_count, count_all.at[half], table_sem.at[1])
    for copy in (own_matrix, own_index, own_count):
        copy.start()
    for copy in inputs:
        copy.wait()

    def pack(site):
        for week in range(weeks_here):
            row = pl.ds(site * rows_here * weeks_here + week, rows_here, stride=weeks_here)
            now = latent[row, :]
            rate = jnp.exp(log_offset[row, :] + now)
            packed[site, 0, week] = now
            packed[site, 1, week] = rate
            packed[site, 2, week] = case_counts[row, :].astype(jnp.float32) - rate

    for peer in range(peers):
        pack(peer * per_chip)

    pl.semaphore_wait(barrier, peers * areas - 1)

    twin = {"ar": 1 - half}
    twin_rows = pl.ds((1 - half) * rows_here, rows_here)
    to_twin = [
        pltpu.make_async_remote_copy(
            slot_index, index_all.at[half], table_sem.at[2], table_sem.at[3], device_id=twin, device_id_type=MESH
        ),
        pltpu.make_async_remote_copy(
            slot_count, count_all.at[half], table_sem.at[4], table_sem.at[5], device_id=twin, device_id_type=MESH
        ),
        pltpu.make_async_remote_copy(
            blocks, matrix.at[own_rows], matrix_sem.at[1], matrix_sem.at[2], device_id=twin, device_id_type=MESH
        ),
    ]
    for copy in to_twin:
        copy.start()

    def scatter(j, step, starting):
        core, slot = j // site_slots, j % site_slots
        peer = lax.rem(me + step, peers)
        site = peer * per_chip + j
        source, target = packed.at[site], field.at[slot, me, half]
        arrived = recv_sem.at[slot, me, half]

        def away():
            copy = pltpu.make_async_remote_copy(
                source, target, send_sem.at[j, step], arrived,
                device_id={"wk": peer, "ar": core}, device_id_type=MESH,
            )
            copy.start() if starting else copy.wait_send()

        def here():
            pltpu.make_async_copy(source, target, arrived).start()

        if step == 0:
            pl.when(half != core)(away)
            if starting:
                pl.when(half == core)(here)
        else:
            away()

    for j in range(per_chip):
        if j > 0:
            for peer in range(peers):
                pack(peer * per_chip + j)
        for step in range(peers):
            scatter(j, step, True)

    def spread(block_row):
        for slot in range(slot_total):
            live = slot < count_all[block_row // rows_here, lax.rem(block_row, rows_here)]
            block = jnp.where(live, matrix[block_row, slot], 0.0)
            high = block.astype(jnp.bfloat16)
            low = (block - high.astype(jnp.float32)).astype(jnp.bfloat16)
            wide[block_row, slot * width : (slot + 1) * width, 0:width] = high
            wide[block_row, slot * width : (slot + 1) * width, width : 2 * width] = low

    own_matrix.wait()
    own_index.wait()
    own_count.wait()

    @pl.loop(0, rows_here)
    def _(n):
        spread(half * rows_here + n)

    for copy in to_twin:
        copy.wait_recv()

    @pl.loop(0, rows_here)
    def _(n):
        spread((1 - half) * rows_here + n)

    def prior(first_lag, second_lag):
        for a in range(areas):
            part = [direction[pl.ds(t * rows + a * rows_here, rows_here), :] for t in range(weeks)]
            inner = []
            for t in range(weeks):
                value = part[t]
                if t >= 1:
                    value = value - first_lag * part[t - 1]
                if t >= 2:
                    value = value - second_lag * part[t - 2]
                inner.append(value)
            for t in range(weeks):
                value = inner[t]
                if t + 1 < weeks:
                    value = value - first_lag * inner[t + 1]
                if t + 2 < weeks:
                    value = value - second_lag * inner[t + 2]
                temporal_rows[pl.ds(t * rows + a * rows_here, rows_here), :] = value
        for g in range(rows):
            value = temporal_rows[pl.ds(g, weeks, stride=rows), :]
            high = value.astype(jnp.bfloat16)
            operand[g, 0:weeks] = high
            operand[g, weeks : 2 * weeks] = (value - high.astype(jnp.float32)).astype(jnp.bfloat16)
        for n in range(rows):
            a, b = n // rows_here, n % rows_here
            left = jnp.concatenate([operand[index_all[a, s, b]] for s in range(slot_total)], axis=1)
            both = jnp.dot(left, wide[n], preferred_element_type=jnp.float32)
            value = both[0:weeks, 0:width] + (both[0:weeks, width:] + both[weeks:, 0:width])
            product[pl.ds(n, weeks, stride=rows), :] = value

    def total(values):
        return jnp.sum(values, axis=(0, 1), keepdims=True)

    def give(slot, step, a, starting):
        peer = lax.rem(me + step, peers)
        source = outgoing.at[slot, peer, a]
        site = me * per_chip + half * site_slots + slot
        target, arrived = returned.at[site], return_sem.at[site]

        def away():
            copy = pltpu.make_async_remote_copy(
                source, target, back_sem.at[slot, step, a], arrived,
                device_id={"wk": peer, "ar": a}, device_id_type=MESH,
            )
            copy.start() if starting else copy.wait_send()

        def here():
            pltpu.make_async_copy(source, target, arrived).start()

        if step == 0:
            pl.when(half != a)(away)
            if starting:
                pl.when(half == a)(here)
        else:
            away()

    @pl.loop(0, sites_here)
    def _(slot):
        site = me * per_chip + half * site_slots + slot
        scale, first_lag, second_lag = tau[site], phi_one[site], phi_two[site]
        for w in range(peers):
            for a in range(areas):
                pltpu.make_async_copy(packed.at[0], field.at[slot, w, a], recv_sem.at[slot, w, a]).wait()
        for w in range(peers):
            for a in range(areas):
                for t in range(weeks_here):
                    row = pl.ds((w * weeks_here + t) * rows + a * rows_here, rows_here)
                    direction[row, :] = field[slot, w, a, 0, t]
                    mean[row, :] = field[slot, w, a, 1, t]
                    residual[row, :] = field[slot, w, a, 2, t]
        prior(first_lag, second_lag)
        gradient = residual[...] - scale * product[...]
        residual[...] = gradient
        direction[...] = gradient
        search[...] = jnp.zeros_like(gradient)

        def iteration(_, norm_now):
            prior(first_lag, second_lag)
            image = scale * product[...] + mean[...] * direction[...]
            alpha = norm_now / total(direction[...] * image)
            search[...] += alpha * direction[...]
            after = residual[...] - alpha * image
            residual[...] = after
            norm_next = total(after * after)
            direction[...] = after + (norm_next / norm_now) * direction[...]
            return norm_next

        lax.fori_loop(0, ITERS, iteration, total(gradient * gradient))
        for w in range(peers):
            for a in range(areas):
                for t in range(weeks_here):
                    row = pl.ds((w * weeks_here + t) * rows + a * rows_here, rows_here)
                    outgoing[slot, w, a, t] = search[row, :]
        for step in range(peers):
            for a in range(areas):
                give(slot, step, a, True)

    for j in range(per_chip):
        for w in range(peers):
            site = w * per_chip + j
            pltpu.make_async_copy(outgoing.at[0, 0, 0], returned.at[site], return_sem.at[site]).wait()
            for week in range(weeks_here):
                row = pl.ds(site * rows_here * weeks_here + week, rows_here, stride=weeks_here)
                out[row, :] = latent[row, :] + returned[site, week]

    for copy in to_twin:
        copy.wait_send()
    for j in range(per_chip):
        for step in range(peers):
            scatter(j, step, False)

    @pl.loop(0, sites_here)
    def _(slot):
        for step in range(peers):
            for a in range(areas):
                give(slot, step, a, False)


def by_site(
    peers, areas, latent, log_offset, case_counts, tau, phi_one, phi_two, blocks, block_index, block_count
):
    cancers, weeks_here, areas_here = latent.shape
    rows_here, slot_total, width, _ = blocks.shape
    if cancers % peers or areas != 2 or rows_here % 8 or (peers * weeks_here) % 16:
        return local(latent, log_offset, case_counts, tau, phi_one, phi_two, blocks, block_index, block_count)
    per_chip = cancers // peers
    site_slots = -(-per_chip // areas)
    weeks, rows = peers * weeks_here, areas * rows_here

    def as_rows(value):
        split = value.reshape(cancers, weeks_here, rows_here, width)
        return split.transpose(0, 2, 1, 3).reshape(cancers * rows_here * weeks_here, width)

    f32, bf16 = jnp.float32, jnp.bfloat16
    tile = (weeks_here, rows_here, width)
    plane = pltpu.VMEM((weeks * rows, width), f32)
    dma = pltpu.SemaphoreType.DMA
    flat = (cancers * rows_here * weeks_here, width)
    scalars = pltpu.SMEM((cancers,), f32)
    result = pl.pallas_call(
        functools.partial(site_kernel, peers, areas, per_chip, weeks_here, rows_here, slot_total),
        out_shape=jax.ShapeDtypeStruct(flat, f32),
        in_specs=[pl.BlockSpec(memory_space=pltpu.HBM)] * 9,
        out_specs=pl.BlockSpec(memory_space=pltpu.VMEM),
        scratch_shapes=[
            pltpu.VMEM(flat, f32), pltpu.VMEM(flat, f32), pltpu.VMEM(flat, jnp.int32), scalars, scalars, scalars,
            pltpu.VMEM((cancers, 3) + tile, f32),
            pltpu.VMEM((site_slots, peers, areas, 3) + tile, f32),
            pltpu.VMEM((rows, slot_total, width, width), f32),
            pltpu.VMEM((rows, slot_total * width, 2 * width), bf16),
            pltpu.SMEM((areas, slot_total, rows_here), jnp.int32),
            pltpu.SMEM((areas, rows_here), jnp.int32),
            plane,
            pltpu.VMEM((rows, 2 * weeks, width), bf16),
            plane, plane, plane, plane, plane,
            pltpu.VMEM((site_slots, peers, areas) + tile, f32),
            pltpu.VMEM((cancers,) + tile, f32),
            dma((6,)),
            dma((per_chip, peers)),
            dma((site_slots, peers, areas)),
            dma((3,)),
            dma((6,)),
            dma((site_slots, peers, areas)),
            dma((cancers,)),
        ],
        compiler_params=pltpu.CompilerParams(
            collective_id=0, has_side_effects=True, vmem_limit_bytes=60 * 1024 * 1024
        ),
    )(
        as_rows(latent), as_rows(log_offset), as_rows(case_counts), tau, phi_one, phi_two,
        blocks, block_index.T, block_count,
    )
    split = result.reshape(cancers, rows_here, weeks_here, width).transpose(0, 2, 1, 3)
    return split.reshape(latent.shape)


def solution(mesh):
    return jax.shard_map(
        functools.partial(by_site, mesh.shape["wk"], mesh.shape["ar"]),
        mesh=mesh,
        in_specs=(
            P("grp", "wk", "ar"),
            P("grp", "wk", "ar"),
            P("grp", "wk", "ar"),
            P(),
            P(),
            P(),
            P("ar", None, None, None),
            P("ar", None),
            P("ar"),
        ),
        out_specs=P("grp", "wk", "ar"),
        check_vma=False,
    )
```

```python
import functools

import jax
import jax.numpy as jnp
from jax import lax
from jax.experimental import pallas as pl
from jax.experimental.pallas import tpu as pltpu
from jax.sharding import PartitionSpec as P

ITERS = 3
MESH = pl.DeviceIdType.MESH


def extended(value, sides, width):
    for axis, dim in sides:
        peers, length = (lax.axis_size(axis), value.shape[dim])
        up = [(i, (i + 1) % peers) for i in range(peers - 1)]
        down = [(j, i) for i, j in up]
        last = lax.slice_in_dim(value, length - width, length, axis=dim)
        initial = lax.slice_in_dim(value, 0, width, axis=dim)
        before = lax.ppermute(last, axis, up)
        after = lax.ppermute(initial, axis, down)
        value = jnp.concatenate([before, value, after], axis=dim)
    return value


def temporal(field, first_lag, second_lag):
    weeks_here = field.shape[1]
    weeks_total = lax.axis_size("wk") * weeks_here
    padded = extended(field, (("wk", 1),), 2)
    innovation = (
        padded[:, 2 : weeks_here + 4]
        - first_lag * padded[:, 1 : weeks_here + 3]
        - second_lag * padded[:, 0 : weeks_here + 2]
    )
    week_number = lax.axis_index("wk") * weeks_here + jnp.arange(weeks_here + 2)
    innovation = jnp.where((week_number < weeks_total)[None, :, None], innovation, 0.0)
    return (
        innovation[:, 0:weeks_here]
        - first_lag * innovation[:, 1 : weeks_here + 1]
        - second_lag * innovation[:, 2 : weeks_here + 2]
    )


def spatial(field, masked, block_index):
    cancers, weeks_here, areas_here = field.shape
    rows_here, slot_total, width, unused = masked.shape
    padded = extended(field, (("ar", 2),), 2 * width)
    first_row = lax.axis_index("ar") * rows_here - 2
    local_index = block_index - first_row
    blocks_of = padded.reshape(cancers, weeks_here, rows_here + 4, width)[:, :, local_index, :]
    result = jnp.einsum("cwnsi,nsij->cwnj", blocks_of, masked, precision=lax.Precision.HIGHEST)
    return result.reshape(cancers, weeks_here, areas_here)


def global_sum(values):
    return lax.psum(values, ("wk", "ar"))[:, None, None]


def local(latent, log_offset, case_counts, tau, phi_one, phi_two, blocks, block_index, block_count):
    slot_live = (jnp.arange(blocks.shape[1])[None, :] < block_count[:, None]).astype(jnp.float32)
    masked = blocks * slot_live[:, :, None, None]
    first_lag = phi_one[:, None, None]
    second_lag = phi_two[:, None, None]
    prior_scale = tau[:, None, None]

    def prior(field):
        return prior_scale * spatial(temporal(field, first_lag, second_lag), masked, block_index)

    mean = jnp.exp(log_offset + latent)
    gradient = case_counts.astype(jnp.float32) - mean - prior(latent)
    search = jnp.zeros_like(latent)
    residual = gradient
    direction = gradient
    norm_now = global_sum(jnp.sum(residual * residual, axis=(1, 2)))
    for iteration in range(ITERS):
        image = prior(direction) + mean * direction
        curve = lax.psum(jnp.sum(direction * image, axis=(1, 2)), ("wk", "ar"))[:, None, None]
        alpha = norm_now / curve
        search = search + alpha * direction
        residual = residual - alpha * image
        norm_next = global_sum(jnp.sum(residual * residual, axis=(1, 2)))
        direction = residual + norm_next / norm_now * direction
        norm_now = norm_next
    return latent + search


def site_kernel(
    peers, areas, per_chip, weeks_here, rows_here, slot_total,
    latent_in, offset_in, counts_in, tau_in, one_in, two_in, blocks, slot_index, slot_count,
    out,
    latent, log_offset, case_counts, tau, phi_one, phi_two,
    packed, field, matrix, wide, index_all, count_all,
    temporal_rows, operand, product, mean, direction, residual, search, outgoing, returned,
    input_sem, send_sem, recv_sem, matrix_sem, table_sem, back_sem, return_sem, known_sem,
):
    me = lax.axis_index("wk")
    half = lax.axis_index("ar")
    width = blocks.shape[-1]
    site_slots = -(-per_chip // areas)
    weeks = peers * weeks_here
    rows = areas * rows_here
    sites_here = jnp.minimum(site_slots, per_chip - half * site_slots)

    levels = peers // 2
    level, column = me // 2, lax.rem(me, 2)
    above, below = levels - 1 - level, level
    barrier = pltpu.get_barrier_semaphore()

    def where_level(far, act):
        if far == 0:
            act()
        else:
            pl.when(above >= far if far > 0 else below >= -far)(act)

    for far in (1, -1, 0):

        def greet(far=far):
            for x in range(2):
                for a in range(areas):

                    def call():
                        pl.semaphore_signal(
                            barrier, inc=1, device_id={"wk": (level + far) * 2 + x, "ar": a}, device_id_type=MESH
                        )

                    if far == 0:
                        pl.when(column * areas + half != x * areas + a)(call)
                    else:
                        call()

        where_level(far, greet)

    inputs = [
        pltpu.make_async_copy(source, target, input_sem.at[n])
        for n, (source, target) in enumerate(
            (
                (latent_in, latent), (offset_in, log_offset), (counts_in, case_counts),
                (tau_in, tau), (one_in, phi_one), (two_in, phi_two),
            )
        )
    ]
    for copy in inputs:
        copy.start()
    own_rows = pl.ds(half * rows_here, rows_here)
    own_matrix = pltpu.make_async_copy(blocks, matrix.at[own_rows], matrix_sem.at[0])
    own_index = pltpu.make_async_copy(slot_index, index_all.at[half], table_sem.at[0])
    own_count = pltpu.make_async_copy(slot_count, count_all.at[half], table_sem.at[1])
    for copy in (own_matrix, own_index, own_count):
        copy.start()
    for copy in inputs:
        copy.wait()

    def pack(site):
        for week in range(weeks_here):
            row = pl.ds(site * rows_here * weeks_here + week, rows_here, stride=weeks_here)
            now = latent[row, :]
            rate = jnp.exp(log_offset[row, :] + now)
            packed[site, 0, week] = now
            packed[site, 1, week] = case_counts[row, :].astype(jnp.float32) - rate
            packed[site, 2, week] = rate

    for peer in range(peers):
        pack(peer * per_chip)

    pl.semaphore_wait(
        barrier, 2 * areas * (1 + jnp.minimum(above, 1) + jnp.minimum(below, 1)) - 1
    )

    def pass_on(far):
        for row, sign in enumerate((1, -1)):
            ahead, behind = (above, below) if sign > 0 else (below, above)

            @pl.when(jnp.minimum(ahead - far, behind - 1) >= 0)
            def _():
                pl.semaphore_signal(
                    known_sem.at[row, far], inc=1,
                    device_id={"wk": (level - sign) * 2 + column}, device_id_type=MESH,
                )

    def learn(far):
        for row, ahead in enumerate((above, below)):

            @pl.when(ahead >= far)
            def _():
                pl.semaphore_wait(known_sem.at[row, far - 1], 1)

    if levels > 2:
        pass_on(1)

    twin = {"ar": 1 - half}
    twin_rows = pl.ds((1 - half) * rows_here, rows_here)
    to_twin = [
        pltpu.make_async_remote_copy(
            slot_index, index_all.at[half], table_sem.at[2], table_sem.at[3], device_id=twin, device_id_type=MESH
        ),
        pltpu.make_async_remote_copy(
            slot_count, count_all.at[half], table_sem.at[4], table_sem.at[5], device_id=twin, device_id_type=MESH
        ),
        pltpu.make_async_remote_copy(
            blocks, matrix.at[own_rows], matrix_sem.at[1], matrix_sem.at[2], device_id=twin, device_id_type=MESH
        ),
    ]

    def scatter(j, part, far, starting):
        core, slot = j // site_slots, j % site_slots
        halves = pl.ds(0, 2) if part == 0 else pl.ds(2, 1)

        def across():
            for x in range(2):
                peer = (level + far) * 2 + x
                source = packed.at[peer * per_chip + j, halves]
                target, arrived = field.at[slot, me, half, halves], recv_sem.at[slot, me, half, part]

                def away():
                    copy = pltpu.make_async_remote_copy(
                        source, target, send_sem.at[j, part, far + levels - 1, x], arrived,
                        device_id={"wk": peer, "ar": core}, device_id_type=MESH,
                    )
                    copy.start() if starting else copy.wait_send()

                def here():
                    pltpu.make_async_copy(source, target, arrived).start()

                if far == 0:
                    mine = column * areas + half == x * areas + core
                    pl.when(jnp.logical_not(mine))(away)
                    if starting:
                        pl.when(mine)(here)
                else:
                    away()

        where_level(far, across)

    def both_ways(far):
        return (far, -far) if far else (0,)

    for far in range(levels):
        if far >= 2:
            learn(far)
            if far < levels - 1:
                pass_on(far)
        for way in both_ways(far):
            scatter(0, 0, way, True)
    for copy in to_twin:
        copy.start()
    far_first = [way for far in range(levels - 1, -1, -1) for way in both_ways(far)]
    for way in far_first:
        scatter(0, 1, way, True)
    for j in range(1, per_chip):
        for peer in range(peers):
            pack(peer * per_chip + j)
        for part in range(2):
            for way in far_first:
                scatter(j, part, way, True)

    def spread(block_row):
        for slot in range(slot_total):
            live = slot < count_all[block_row // rows_here, lax.rem(block_row, rows_here)]
            block = jnp.where(live, matrix[block_row, slot], 0.0)
            high = block.astype(jnp.bfloat16)
            low = (block - high.astype(jnp.float32)).astype(jnp.bfloat16)
            wide[block_row, slot * width : (slot + 1) * width, 0:width] = high
            wide[block_row, slot * width : (slot + 1) * width, width : 2 * width] = low

    own_matrix.wait()
    own_index.wait()
    own_count.wait()

    @pl.loop(0, rows_here)
    def _(n):
        spread(half * rows_here + n)

    for copy in to_twin:
        copy.wait_recv()

    @pl.loop(0, rows_here)
    def _(n):
        spread((1 - half) * rows_here + n)

    def prior(first_lag, second_lag):
        for a in range(areas):
            part = [direction[pl.ds(t * rows + a * rows_here, rows_here), :] for t in range(weeks)]
            inner = []
            for t in range(weeks):
                value = part[t]
                if t >= 1:
                    value = value - first_lag * part[t - 1]
                if t >= 2:
                    value = value - second_lag * part[t - 2]
                inner.append(value)
            for t in range(weeks):
                value = inner[t]
                if t + 1 < weeks:
                    value = value - first_lag * inner[t + 1]
                if t + 2 < weeks:
                    value = value - second_lag * inner[t + 2]
                temporal_rows[pl.ds(t * rows + a * rows_here, rows_here), :] = value
        for g in range(rows):
            value = temporal_rows[pl.ds(g, weeks, stride=rows), :]
            high = value.astype(jnp.bfloat16)
            operand[g, 0:weeks] = high
            operand[g, weeks : 2 * weeks] = (value - high.astype(jnp.float32)).astype(jnp.bfloat16)
        for n in range(rows):
            a, b = n // rows_here, n % rows_here
            left = jnp.concatenate([operand[index_all[a, s, b]] for s in range(slot_total)], axis=1)
            both = jnp.dot(left, wide[n], preferred_element_type=jnp.float32)
            value = both[0:weeks, 0:width] + (both[0:weeks, width:] + both[weeks:, 0:width])
            product[pl.ds(n, weeks, stride=rows), :] = value

    def total(values):
        return jnp.sum(values, axis=(0, 1), keepdims=True)

    def give(slot, far, starting):
        site = me * per_chip + half * site_slots + slot
        target, arrived = returned.at[site], return_sem.at[site]

        def across():
            for x in range(2):
                for a in range(areas):
                    peer = (level + far) * 2 + x
                    source = outgoing.at[slot, peer, a]

                    def away():
                        copy = pltpu.make_async_remote_copy(
                            source, target, back_sem.at[slot, far + levels - 1, x, a], arrived,
                            device_id={"wk": peer, "ar": a}, device_id_type=MESH,
                        )
                        copy.start() if starting else copy.wait_send()

                    def here():
                        pltpu.make_async_copy(source, target, arrived).start()

                    if far == 0:
                        mine = column * areas + half == x * areas + a
                        pl.when(jnp.logical_not(mine))(away)
                        if starting:
                            pl.when(mine)(here)
                    else:
                        away()

        where_level(far, across)

    def take(slot, part):
        halves = pl.ds(0, 2) if part == 0 else pl.ds(2, 1)
        for w in range(peers):
            for a in range(areas):
                pltpu.make_async_copy(
                    packed.at[0, halves], field.at[slot, w, a, halves], recv_sem.at[slot, w, a, part]
                ).wait()

    def unpack(slot, number, target):
        for w in range(peers):
            for a in range(areas):
                for t in range(weeks_here):
                    row = pl.ds((w * weeks_here + t) * rows + a * rows_here, rows_here)
                    target[row, :] = field[slot, w, a, number, t]

    @pl.loop(0, sites_here)
    def _(slot):
        site = me * per_chip + half * site_slots + slot
        scale, first_lag, second_lag = tau[site], phi_one[site], phi_two[site]
        take(slot, 0)
        unpack(slot, 0, direction)
        unpack(slot, 1, residual)
        prior(first_lag, second_lag)
        gradient = residual[...] - scale * product[...]
        residual[...] = gradient
        direction[...] = gradient
        search[...] = jnp.zeros_like(gradient)
        prior(first_lag, second_lag)
        take(slot, 1)
        unpack(slot, 2, mean)

        def step_length(norm_now):
            image = scale * product[...] + mean[...] * direction[...]
            return image, norm_now / total(direction[...] * image)

        def iteration(_, norm_now):
            image, alpha = step_length(norm_now)
            search[...] += alpha * direction[...]
            after = residual[...] - alpha * image
            residual[...] = after
            norm_next = total(after * after)
            direction[...] = after + (norm_next / norm_now) * direction[...]
            prior(first_lag, second_lag)
            return norm_next

        norm_last = lax.fori_loop(0, ITERS - 1, iteration, total(gradient * gradient))
        _, alpha = step_length(norm_last)
        search[...] += alpha * direction[...]
        for w in range(peers):
            for a in range(areas):
                for t in range(weeks_here):
                    row = pl.ds((w * weeks_here + t) * rows + a * rows_here, rows_here)
                    outgoing[slot, w, a, t] = search[row, :]
        for way in far_first:
            give(slot, way, True)

    for j in range(per_chip):
        for w in range(peers):
            site = w * per_chip + j
            pltpu.make_async_copy(outgoing.at[0, 0, 0], returned.at[site], return_sem.at[site]).wait()
            for week in range(weeks_here):
                row = pl.ds(site * rows_here * weeks_here + week, rows_here, stride=weeks_here)
                out[row, :] = latent[row, :] + returned[site, week]

    for copy in to_twin:
        copy.wait_send()
    for j in range(per_chip):
        for part in range(2):
            for way in far_first:
                scatter(j, part, way, False)

    @pl.loop(0, sites_here)
    def _(slot):
        for way in far_first:
            give(slot, way, False)


def by_site(
    peers, areas, latent, log_offset, case_counts, tau, phi_one, phi_two, blocks, block_index, block_count
):
    cancers, weeks_here, areas_here = latent.shape
    rows_here, slot_total, width, _ = blocks.shape
    if cancers % peers or peers % 2 or areas != 2 or rows_here % 8 or (peers * weeks_here) % 16:
        return local(latent, log_offset, case_counts, tau, phi_one, phi_two, blocks, block_index, block_count)
    per_chip = cancers // peers
    site_slots = -(-per_chip // areas)
    weeks, rows = peers * weeks_here, areas * rows_here

    def as_rows(value):
        split = value.reshape(cancers, weeks_here, rows_here, width)
        return split.transpose(0, 2, 1, 3).reshape(cancers * rows_here * weeks_here, width)

    f32, bf16 = jnp.float32, jnp.bfloat16
    tile = (weeks_here, rows_here, width)
    plane = pltpu.VMEM((weeks * rows, width), f32)
    dma = pltpu.SemaphoreType.DMA
    flat = (cancers * rows_here * weeks_here, width)
    scalars = pltpu.SMEM((cancers,), f32)
    result = pl.pallas_call(
        functools.partial(site_kernel, peers, areas, per_chip, weeks_here, rows_here, slot_total),
        out_shape=jax.ShapeDtypeStruct(flat, f32),
        in_specs=[pl.BlockSpec(memory_space=pltpu.HBM)] * 9,
        out_specs=pl.BlockSpec(memory_space=pltpu.VMEM),
        scratch_shapes=[
            pltpu.VMEM(flat, f32), pltpu.VMEM(flat, f32), pltpu.VMEM(flat, jnp.int32), scalars, scalars, scalars,
            pltpu.VMEM((cancers, 3) + tile, f32),
            pltpu.VMEM((site_slots, peers, areas, 3) + tile, f32),
            pltpu.VMEM((rows, slot_total, width, width), f32),
            pltpu.VMEM((rows, slot_total * width, 2 * width), bf16),
            pltpu.SMEM((areas, slot_total, rows_here), jnp.int32),
            pltpu.SMEM((areas, rows_here), jnp.int32),
            plane,
            pltpu.VMEM((rows, 2 * weeks, width), bf16),
            plane, plane, plane, plane, plane,
            pltpu.VMEM((site_slots, peers, areas) + tile, f32),
            pltpu.VMEM((cancers,) + tile, f32),
            dma((6,)),
            dma((per_chip, 2, peers - 1, 2)),
            dma((site_slots, peers, areas, 2)),
            dma((3,)),
            dma((6,)),
            dma((site_slots, peers - 1, 2, areas)),
            dma((cancers,)),
            pltpu.SemaphoreType.REGULAR((2, peers // 2)),
        ],
        compiler_params=pltpu.CompilerParams(
            collective_id=0, has_side_effects=True, vmem_limit_bytes=60 * 1024 * 1024
        ),
    )(
        as_rows(latent), as_rows(log_offset), as_rows(case_counts), tau, phi_one, phi_two,
        blocks, block_index.T, block_count,
    )
    split = result.reshape(cancers, rows_here, weeks_here, width).transpose(0, 2, 1, 3)
    return split.reshape(latent.shape)


def solution(mesh):
    return jax.shard_map(
        functools.partial(by_site, mesh.shape["wk"], mesh.shape["ar"]),
        mesh=mesh,
        in_specs=(
            P("grp", "wk", "ar"),
            P("grp", "wk", "ar"),
            P("grp", "wk", "ar"),
            P(),
            P(),
            P(),
            P("ar", None, None, None),
            P("ar", None),
            P("ar"),
        ),
        out_specs=P("grp", "wk", "ar"),
        check_vma=False,
    )
```

```python
import functools

import jax
import jax.numpy as jnp
from jax import lax
from jax.experimental import pallas as pl
from jax.experimental.pallas import tpu as pltpu
from jax.sharding import PartitionSpec as P

ITERS = 3
MESH = pl.DeviceIdType.MESH


def extended(value, sides, width):
    for axis, dim in sides:
        peers, length = (lax.axis_size(axis), value.shape[dim])
        up = [(i, (i + 1) % peers) for i in range(peers - 1)]
        down = [(j, i) for i, j in up]
        last = lax.slice_in_dim(value, length - width, length, axis=dim)
        initial = lax.slice_in_dim(value, 0, width, axis=dim)
        before = lax.ppermute(last, axis, up)
        after = lax.ppermute(initial, axis, down)
        value = jnp.concatenate([before, value, after], axis=dim)
    return value


def temporal(field, first_lag, second_lag):
    weeks_here = field.shape[1]
    weeks_total = lax.axis_size("wk") * weeks_here
    padded = extended(field, (("wk", 1),), 2)
    innovation = (
        padded[:, 2 : weeks_here + 4]
        - first_lag * padded[:, 1 : weeks_here + 3]
        - second_lag * padded[:, 0 : weeks_here + 2]
    )
    week_number = lax.axis_index("wk") * weeks_here + jnp.arange(weeks_here + 2)
    innovation = jnp.where((week_number < weeks_total)[None, :, None], innovation, 0.0)
    return (
        innovation[:, 0:weeks_here]
        - first_lag * innovation[:, 1 : weeks_here + 1]
        - second_lag * innovation[:, 2 : weeks_here + 2]
    )


def spatial(field, masked, block_index):
    cancers, weeks_here, areas_here = field.shape
    rows_here, slot_total, width, unused = masked.shape
    padded = extended(field, (("ar", 2),), 2 * width)
    first_row = lax.axis_index("ar") * rows_here - 2
    local_index = block_index - first_row
    blocks_of = padded.reshape(cancers, weeks_here, rows_here + 4, width)[:, :, local_index, :]
    result = jnp.einsum("cwnsi,nsij->cwnj", blocks_of, masked, precision=lax.Precision.HIGHEST)
    return result.reshape(cancers, weeks_here, areas_here)


def global_sum(values):
    return lax.psum(values, ("wk", "ar"))[:, None, None]


def local(latent, log_offset, case_counts, tau, phi_one, phi_two, blocks, block_index, block_count):
    slot_live = (jnp.arange(blocks.shape[1])[None, :] < block_count[:, None]).astype(jnp.float32)
    masked = blocks * slot_live[:, :, None, None]
    first_lag = phi_one[:, None, None]
    second_lag = phi_two[:, None, None]
    prior_scale = tau[:, None, None]

    def prior(field):
        return prior_scale * spatial(temporal(field, first_lag, second_lag), masked, block_index)

    mean = jnp.exp(log_offset + latent)
    gradient = case_counts.astype(jnp.float32) - mean - prior(latent)
    search = jnp.zeros_like(latent)
    residual = gradient
    direction = gradient
    norm_now = global_sum(jnp.sum(residual * residual, axis=(1, 2)))
    for iteration in range(ITERS):
        image = prior(direction) + mean * direction
        curve = lax.psum(jnp.sum(direction * image, axis=(1, 2)), ("wk", "ar"))[:, None, None]
        alpha = norm_now / curve
        search = search + alpha * direction
        residual = residual - alpha * image
        norm_next = global_sum(jnp.sum(residual * residual, axis=(1, 2)))
        direction = residual + norm_next / norm_now * direction
        norm_now = norm_next
    return latent + search


def site_kernel(
    peers, areas, per_chip, weeks_here, rows_here, slot_total,
    latent_in, offset_in, counts_in, tau_in, one_in, two_in, blocks, slot_index, slot_count,
    out,
    latent, log_offset, case_counts, tau, phi_one, phi_two,
    packed, field, matrix, wide, index_all, count_all,
    temporal_rows, operand, product, mean, direction, residual, search, outgoing, returned,
    input_sem, send_sem, recv_sem, matrix_sem, table_sem, back_sem, return_sem, known_sem,
):
    me = lax.axis_index("wk")
    half = lax.axis_index("ar")
    width = blocks.shape[-1]
    site_slots = -(-per_chip // areas)
    weeks = peers * weeks_here
    rows = areas * rows_here
    sites_here = jnp.minimum(site_slots, per_chip - half * site_slots)

    levels = peers // 2
    level, column = me // 2, lax.rem(me, 2)
    above, below = levels - 1 - level, level
    barrier = pltpu.get_barrier_semaphore()

    def where_level(far, act):
        if far == 0:
            act()
        else:
            pl.when(above >= far if far > 0 else below >= -far)(act)

    for far in (1, -1, 0):

        def greet(far=far):
            for x in range(2):
                for a in range(areas):

                    def call():
                        pl.semaphore_signal(
                            barrier, inc=1, device_id={"wk": (level + far) * 2 + x, "ar": a}, device_id_type=MESH
                        )

                    if far == 0:
                        pl.when(column * areas + half != x * areas + a)(call)
                    else:
                        call()

        where_level(far, greet)

    inputs = [
        pltpu.make_async_copy(source, target, input_sem.at[n])
        for n, (source, target) in enumerate(
            (
                (latent_in, latent), (offset_in, log_offset), (counts_in, case_counts),
                (tau_in, tau), (one_in, phi_one), (two_in, phi_two),
            )
        )
    ]
    for copy in inputs:
        copy.start()
    own_rows = pl.ds(half * rows_here, rows_here)
    own_matrix = pltpu.make_async_copy(blocks, matrix.at[own_rows], matrix_sem.at[0])
    own_index = pltpu.make_async_copy(slot_index, index_all.at[half], table_sem.at[0])
    own_count = pltpu.make_async_copy(slot_count, count_all.at[half], table_sem.at[1])
    for copy in (own_matrix, own_index, own_count):
        copy.start()
    for copy in inputs:
        copy.wait()

    def pack(site):
        for week in range(weeks_here):
            row = pl.ds(site * rows_here * weeks_here + week, rows_here, stride=weeks_here)
            now = latent[row, :]
            rate = jnp.exp(log_offset[row, :] + now)
            packed[site, 0, week] = now
            packed[site, 1, week] = case_counts[row, :].astype(jnp.float32) - rate
            packed[site, 2, week] = rate

    for peer in range(peers):
        pack(peer * per_chip)

    pl.semaphore_wait(
        barrier, 2 * areas * (1 + jnp.minimum(above, 1) + jnp.minimum(below, 1)) - 1
    )

    def pass_on(far):
        for row, sign in enumerate((1, -1)):
            ahead, behind = (above, below) if sign > 0 else (below, above)

            @pl.when(jnp.minimum(ahead - far, behind - 1) >= 0)
            def _():
                pl.semaphore_signal(
                    known_sem.at[row, far], inc=1,
                    device_id={"wk": (level - sign) * 2 + column}, device_id_type=MESH,
                )

    def learn(far):
        for row, ahead in enumerate((above, below)):

            @pl.when(ahead >= far)
            def _():
                pl.semaphore_wait(known_sem.at[row, far - 1], 1)

    if levels > 2:
        pass_on(1)

    twin = {"ar": 1 - half}
    twin_rows = pl.ds((1 - half) * rows_here, rows_here)
    to_twin = [
        pltpu.make_async_remote_copy(
            slot_index, index_all.at[half], table_sem.at[2], table_sem.at[3], device_id=twin, device_id_type=MESH
        ),
        pltpu.make_async_remote_copy(
            slot_count, count_all.at[half], table_sem.at[4], table_sem.at[5], device_id=twin, device_id_type=MESH
        ),
        pltpu.make_async_remote_copy(
            blocks, matrix.at[own_rows], matrix_sem.at[1], matrix_sem.at[2], device_id=twin, device_id_type=MESH
        ),
    ]

    def scatter(j, part, far, starting):
        core, slot = j // site_slots, j % site_slots
        halves = pl.ds(0, 2) if part == 0 else pl.ds(2, 1)

        def across():
            for x in range(2):
                peer = (level + far) * 2 + x
                source = packed.at[peer * per_chip + j, halves]
                target, arrived = field.at[slot, me, half, halves], recv_sem.at[slot, me, half, part]

                def away():
                    copy = pltpu.make_async_remote_copy(
                        source, target, send_sem.at[j, part, far + levels - 1, x], arrived,
                        device_id={"wk": peer, "ar": core}, device_id_type=MESH,
                    )
                    copy.start() if starting else copy.wait_send()

                def here():
                    pltpu.make_async_copy(source, target, arrived).start()

                if far == 0:
                    mine = column * areas + half == x * areas + core
                    pl.when(jnp.logical_not(mine))(away)
                    if starting:
                        pl.when(mine)(here)
                else:
                    away()

        where_level(far, across)

    def both_ways(far):
        return (far, -far) if far else (0,)

    for far in range(levels):
        if far >= 2:
            learn(far)
            if far < levels - 1:
                pass_on(far)
        for way in both_ways(far):
            scatter(0, 0, way, True)
    for copy in to_twin:
        copy.start()
    far_first = [way for far in range(levels - 1, -1, -1) for way in both_ways(far)]
    for way in far_first:
        scatter(0, 1, way, True)
    for j in range(1, per_chip):
        for peer in range(peers):
            pack(peer * per_chip + j)
        for part in range(2):
            for way in far_first:
                scatter(j, part, way, True)

    def spread(block_row):
        for slot in range(slot_total):
            live = slot < count_all[block_row // rows_here, lax.rem(block_row, rows_here)]
            block = jnp.where(live, matrix[block_row, slot], 0.0)
            high = block.astype(jnp.bfloat16)
            low = (block - high.astype(jnp.float32)).astype(jnp.bfloat16)
            wide[block_row, slot * width : (slot + 1) * width, 0:width] = high
            wide[block_row, slot * width : (slot + 1) * width, width : 2 * width] = low

    own_matrix.wait()
    own_index.wait()
    own_count.wait()

    @pl.loop(0, rows_here)
    def _(n):
        spread(half * rows_here + n)

    for copy in to_twin:
        copy.wait_recv()

    @pl.loop(0, rows_here)
    def _(n):
        spread((1 - half) * rows_here + n)

    def prior(first_lag, second_lag):
        for a in range(areas):
            part = [direction[pl.ds(t * rows + a * rows_here, rows_here), :] for t in range(weeks)]
            inner = []
            for t in range(weeks):
                value = part[t]
                if t >= 1:
                    value = value - first_lag * part[t - 1]
                if t >= 2:
                    value = value - second_lag * part[t - 2]
                inner.append(value)
            for t in range(weeks):
                value = inner[t]
                if t + 1 < weeks:
                    value = value - first_lag * inner[t + 1]
                if t + 2 < weeks:
                    value = value - second_lag * inner[t + 2]
                temporal_rows[pl.ds(t * rows + a * rows_here, rows_here), :] = value
        for g in range(rows):
            value = temporal_rows[pl.ds(g, weeks, stride=rows), :]
            high = value.astype(jnp.bfloat16)
            operand[g, 0:weeks] = high
            operand[g, weeks : 2 * weeks] = (value - high.astype(jnp.float32)).astype(jnp.bfloat16)
        for n in range(rows):
            a, b = n // rows_here, n % rows_here
            left = jnp.concatenate([operand[index_all[a, s, b]] for s in range(slot_total)], axis=1)
            both = jnp.dot(left, wide[n], preferred_element_type=jnp.float32)
            value = both[0:weeks, 0:width] + (both[0:weeks, width:] + both[weeks:, 0:width])
            product[pl.ds(n, weeks, stride=rows), :] = value

    def total(values):
        return jnp.sum(values, axis=(0, 1), keepdims=True)

    def give(slot, far, starting):
        site = me * per_chip + half * site_slots + slot
        target, arrived = returned.at[site], return_sem.at[site]

        def across():
            for x in range(2):
                for a in range(areas):
                    peer = (level + far) * 2 + x
                    source = outgoing.at[slot, peer, a]

                    def away():
                        copy = pltpu.make_async_remote_copy(
                            source, target, back_sem.at[slot, far + levels - 1, x, a], arrived,
                            device_id={"wk": peer, "ar": a}, device_id_type=MESH,
                        )
                        copy.start() if starting else copy.wait_send()

                    def here():
                        pltpu.make_async_copy(source, target, arrived).start()

                    if far == 0:
                        mine = column * areas + half == x * areas + a
                        pl.when(jnp.logical_not(mine))(away)
                        if starting:
                            pl.when(mine)(here)
                    else:
                        away()

        where_level(far, across)

    def take(slot, part):
        halves = pl.ds(0, 2) if part == 0 else pl.ds(2, 1)
        for w in range(peers):
            for a in range(areas):
                pltpu.make_async_copy(
                    packed.at[0, halves], field.at[slot, w, a, halves], recv_sem.at[slot, w, a, part]
                ).wait()

    def unpack(slot, number, target):
        for w in range(peers):
            for a in range(areas):
                for t in range(weeks_here):
                    row = pl.ds((w * weeks_here + t) * rows + a * rows_here, rows_here)
                    target[row, :] = field[slot, w, a, number, t]

    @pl.loop(0, sites_here)
    def _(slot):
        site = me * per_chip + half * site_slots + slot
        scale, first_lag, second_lag = tau[site], phi_one[site], phi_two[site]
        take(slot, 0)
        unpack(slot, 0, direction)
        unpack(slot, 1, residual)
        prior(first_lag, second_lag)
        gradient = residual[...] - scale * product[...]
        residual[...] = gradient
        direction[...] = gradient
        search[...] = jnp.zeros_like(gradient)
        prior(first_lag, second_lag)
        take(slot, 1)
        unpack(slot, 2, mean)

        def step_length(norm_now):
            image = scale * product[...] + mean[...] * direction[...]
            return image, norm_now / total(direction[...] * image)

        def iteration(_, norm_now):
            image, alpha = step_length(norm_now)
            search[...] += alpha * direction[...]
            after = residual[...] - alpha * image
            residual[...] = after
            norm_next = total(after * after)
            direction[...] = after + (norm_next / norm_now) * direction[...]
            prior(first_lag, second_lag)
            return norm_next

        norm_last = lax.fori_loop(0, ITERS - 1, iteration, total(gradient * gradient))
        _, alpha = step_length(norm_last)
        search[...] += alpha * direction[...]
        for w in range(peers):
            for a in range(areas):
                for t in range(weeks_here):
                    row = pl.ds((w * weeks_here + t) * rows + a * rows_here, rows_here)
                    outgoing[slot, w, a, t] = search[row, :]
        for way in far_first:
            give(slot, way, True)

    for j in range(per_chip):
        for w in range(peers):
            site = w * per_chip + j
            pltpu.make_async_copy(outgoing.at[0, 0, 0], returned.at[site], return_sem.at[site]).wait()
            for week in range(weeks_here):
                row = pl.ds(site * rows_here * weeks_here + week, rows_here, stride=weeks_here)
                out[row, :] = latent[row, :] + returned[site, week]

    for copy in to_twin:
        copy.wait_send()
    for j in range(per_chip):
        for part in range(2):
            for way in far_first:
                scatter(j, part, way, False)

    @pl.loop(0, sites_here)
    def _(slot):
        for way in far_first:
            give(slot, way, False)


def by_site(
    peers, areas, latent, log_offset, case_counts, tau, phi_one, phi_two, blocks, block_index, block_count
):
    cancers, weeks_here, areas_here = latent.shape
    rows_here, slot_total, width, _ = blocks.shape
    if cancers % peers or peers % 2 or areas != 2 or rows_here % 8 or (peers * weeks_here) % 16:
        return local(latent, log_offset, case_counts, tau, phi_one, phi_two, blocks, block_index, block_count)
    per_chip = cancers // peers
    site_slots = -(-per_chip // areas)
    weeks, rows = peers * weeks_here, areas * rows_here

    def as_rows(value):
        split = value.reshape(cancers, weeks_here, rows_here, width)
        return split.transpose(0, 2, 1, 3).reshape(cancers * rows_here * weeks_here, width)

    f32, bf16 = jnp.float32, jnp.bfloat16
    tile = (weeks_here, rows_here, width)
    plane = pltpu.VMEM((weeks * rows, width), f32)
    dma = pltpu.SemaphoreType.DMA
    flat = (cancers * rows_here * weeks_here, width)
    scalars = pltpu.SMEM((cancers,), f32)
    operands = (
        as_rows(latent), as_rows(log_offset), as_rows(case_counts), tau, phi_one, phi_two,
        blocks, block_index.T, block_count,
    )
    result = pl.pallas_call(
        functools.partial(site_kernel, peers, areas, per_chip, weeks_here, rows_here, slot_total),
        out_shape=pltpu.VMEM(flat, f32),
        in_specs=[pl.BlockSpec(memory_space=pltpu.HBM)] * 9,
        out_specs=pl.BlockSpec(memory_space=pltpu.VMEM),
        scratch_shapes=[
            pltpu.VMEM(flat, f32), pltpu.VMEM(flat, f32), pltpu.VMEM(flat, jnp.int32), scalars, scalars, scalars,
            pltpu.VMEM((cancers, 3) + tile, f32),
            pltpu.VMEM((site_slots, peers, areas, 3) + tile, f32),
            pltpu.VMEM((rows, slot_total, width, width), f32),
            pltpu.VMEM((rows, slot_total * width, 2 * width), bf16),
            pltpu.SMEM((areas, slot_total, rows_here), jnp.int32),
            pltpu.SMEM((areas, rows_here), jnp.int32),
            plane,
            pltpu.VMEM((rows, 2 * weeks, width), bf16),
            plane, plane, plane, plane, plane,
            pltpu.VMEM((site_slots, peers, areas) + tile, f32),
            pltpu.VMEM((cancers,) + tile, f32),
            dma((6,)),
            dma((per_chip, 2, peers - 1, 2)),
            dma((site_slots, peers, areas, 2)),
            dma((3,)),
            dma((6,)),
            dma((site_slots, peers - 1, 2, areas)),
            dma((cancers,)),
            pltpu.SemaphoreType.REGULAR((2, peers // 2)),
        ],
        compiler_params=pltpu.CompilerParams(
            collective_id=0, has_side_effects=True, vmem_limit_bytes=40 * 1024 * 1024
        ),
    )(*(pltpu.with_memory_space_constraint(operand, pltpu.HBM) for operand in operands))
    split = result.reshape(cancers, rows_here, weeks_here, width).transpose(0, 2, 1, 3)
    return split.reshape(latent.shape)


def solution(mesh):
    return jax.shard_map(
        functools.partial(by_site, mesh.shape["wk"], mesh.shape["ar"]),
        mesh=mesh,
        in_specs=(
            P("grp", "wk", "ar"),
            P("grp", "wk", "ar"),
            P("grp", "wk", "ar"),
            P(),
            P(),
            P(),
            P("ar", None, None, None),
            P("ar", None),
            P("ar"),
        ),
        out_specs=P("grp", "wk", "ar"),
        check_vma=False,
    )
```

```python
import functools

import jax
import jax.numpy as jnp
from jax import lax
from jax.experimental import pallas as pl
from jax.experimental.pallas import tpu as pltpu
from jax.sharding import PartitionSpec as P

ITERS = 3
MESH = pl.DeviceIdType.MESH


def extended(value, sides, width):
    for axis, dim in sides:
        peers, length = (lax.axis_size(axis), value.shape[dim])
        up = [(i, (i + 1) % peers) for i in range(peers - 1)]
        down = [(j, i) for i, j in up]
        last = lax.slice_in_dim(value, length - width, length, axis=dim)
        initial = lax.slice_in_dim(value, 0, width, axis=dim)
        before = lax.ppermute(last, axis, up)
        after = lax.ppermute(initial, axis, down)
        value = jnp.concatenate([before, value, after], axis=dim)
    return value


def temporal(field, first_lag, second_lag):
    weeks_here = field.shape[1]
    weeks_total = lax.axis_size("wk") * weeks_here
    padded = extended(field, (("wk", 1),), 2)
    innovation = (
        padded[:, 2 : weeks_here + 4]
        - first_lag * padded[:, 1 : weeks_here + 3]
        - second_lag * padded[:, 0 : weeks_here + 2]
    )
    week_number = lax.axis_index("wk") * weeks_here + jnp.arange(weeks_here + 2)
    innovation = jnp.where((week_number < weeks_total)[None, :, None], innovation, 0.0)
    return (
        innovation[:, 0:weeks_here]
        - first_lag * innovation[:, 1 : weeks_here + 1]
        - second_lag * innovation[:, 2 : weeks_here + 2]
    )


def spatial(field, masked, block_index):
    cancers, weeks_here, areas_here = field.shape
    rows_here, slot_total, width, unused = masked.shape
    padded = extended(field, (("ar", 2),), 2 * width)
    first_row = lax.axis_index("ar") * rows_here - 2
    local_index = block_index - first_row
    blocks_of = padded.reshape(cancers, weeks_here, rows_here + 4, width)[:, :, local_index, :]
    result = jnp.einsum("cwnsi,nsij->cwnj", blocks_of, masked, precision=lax.Precision.HIGHEST)
    return result.reshape(cancers, weeks_here, areas_here)


def global_sum(values):
    return lax.psum(values, ("wk", "ar"))[:, None, None]


def local(latent, log_offset, case_counts, tau, phi_one, phi_two, blocks, block_index, block_count):
    slot_live = (jnp.arange(blocks.shape[1])[None, :] < block_count[:, None]).astype(jnp.float32)
    masked = blocks * slot_live[:, :, None, None]
    first_lag = phi_one[:, None, None]
    second_lag = phi_two[:, None, None]
    prior_scale = tau[:, None, None]

    def prior(field):
        return prior_scale * spatial(temporal(field, first_lag, second_lag), masked, block_index)

    mean = jnp.exp(log_offset + latent)
    gradient = case_counts.astype(jnp.float32) - mean - prior(latent)
    search = jnp.zeros_like(latent)
    residual = gradient
    direction = gradient
    norm_now = global_sum(jnp.sum(residual * residual, axis=(1, 2)))
    for iteration in range(ITERS):
        image = prior(direction) + mean * direction
        curve = lax.psum(jnp.sum(direction * image, axis=(1, 2)), ("wk", "ar"))[:, None, None]
        alpha = norm_now / curve
        search = search + alpha * direction
        residual = residual - alpha * image
        norm_next = global_sum(jnp.sum(residual * residual, axis=(1, 2)))
        direction = residual + norm_next / norm_now * direction
        norm_now = norm_next
    return latent + search


def site_kernel(
    peers, areas, per_chip, weeks_here, rows_here, slot_total,
    latent_in, offset_in, counts_in, tau_in, one_in, two_in, blocks, slot_index, slot_count,
    out,
    latent, log_offset, case_counts, tau, phi_one, phi_two,
    packed, field, matrix, wide, index_all, count_all,
    temporal_rows, operand, product, mean, direction, residual, search, outgoing, returned,
    input_sem, send_sem, recv_sem, matrix_sem, table_sem, back_sem, return_sem, known_sem,
):
    me = lax.axis_index("wk")
    half = lax.axis_index("ar")
    width = blocks.shape[-1]
    site_slots = -(-per_chip // areas)
    weeks = peers * weeks_here
    rows = areas * rows_here
    sites_here = jnp.minimum(site_slots, per_chip - half * site_slots)

    levels = peers // 2
    level, column = me // 2, lax.rem(me, 2)
    above, below = levels - 1 - level, level
    barrier = pltpu.get_barrier_semaphore()

    def where_level(far, act):
        if far == 0:
            act()
        else:
            pl.when(above >= far if far > 0 else below >= -far)(act)

    for far in (1, -1, 0):

        def greet(far=far):
            for x in range(2):
                for a in range(areas):

                    def call():
                        pl.semaphore_signal(
                            barrier, inc=1, device_id={"wk": (level + far) * 2 + x, "ar": a}, device_id_type=MESH
                        )

                    if far == 0:
                        pl.when(column * areas + half != x * areas + a)(call)
                    else:
                        call()

        where_level(far, greet)

    inputs = [
        pltpu.make_async_copy(source, target, input_sem.at[n])
        for n, (source, target) in enumerate(
            (
                (latent_in, latent), (offset_in, log_offset), (counts_in, case_counts),
                (tau_in, tau), (one_in, phi_one), (two_in, phi_two),
            )
        )
    ]
    for copy in inputs:
        copy.start()
    own_rows = pl.ds(half * rows_here, rows_here)
    own_matrix = pltpu.make_async_copy(blocks, matrix.at[own_rows], matrix_sem.at[0])
    own_index = pltpu.make_async_copy(slot_index, index_all.at[half], table_sem.at[0])
    own_count = pltpu.make_async_copy(slot_count, count_all.at[half], table_sem.at[1])
    for copy in (own_matrix, own_index, own_count):
        copy.start()
    for copy in inputs:
        copy.wait()

    def pack(site):
        for week in range(weeks_here):
            row = pl.ds(site * rows_here * weeks_here + week, rows_here, stride=weeks_here)
            now = latent[row, :]
            rate = jnp.exp(log_offset[row, :] + now)
            packed[site, 0, week] = now
            packed[site, 1, week] = case_counts[row, :].astype(jnp.float32) - rate
            packed[site, 2, week] = rate

    for peer in range(peers):
        pack(peer * per_chip)

    pl.semaphore_wait(
        barrier, 2 * areas * (1 + jnp.minimum(above, 1) + jnp.minimum(below, 1)) - 1
    )

    def pass_on(far):
        for row, sign in enumerate((1, -1)):
            ahead, behind = (above, below) if sign > 0 else (below, above)

            @pl.when(jnp.minimum(ahead - far, behind - 1) >= 0)
            def _():
                pl.semaphore_signal(
                    known_sem.at[row, far], inc=1,
                    device_id={"wk": (level - sign) * 2 + column}, device_id_type=MESH,
                )

    def learn(far):
        for row, ahead in enumerate((above, below)):

            @pl.when(ahead >= far)
            def _():
                pl.semaphore_wait(known_sem.at[row, far - 1], 1)

    if levels > 2:
        pass_on(1)

    twin = {"ar": 1 - half}
    twin_rows = pl.ds((1 - half) * rows_here, rows_here)
    to_twin = [
        pltpu.make_async_remote_copy(
            slot_index, index_all.at[half], table_sem.at[2], table_sem.at[3], device_id=twin, device_id_type=MESH
        ),
        pltpu.make_async_remote_copy(
            slot_count, count_all.at[half], table_sem.at[4], table_sem.at[5], device_id=twin, device_id_type=MESH
        ),
        pltpu.make_async_remote_copy(
            blocks, matrix.at[own_rows], matrix_sem.at[1], matrix_sem.at[2], device_id=twin, device_id_type=MESH
        ),
    ]

    def scatter(j, part, far, starting):
        core, slot = j // site_slots, j % site_slots
        halves = pl.ds(part, 1)

        def across():
            for x in range(2):
                peer = (level + far) * 2 + x
                source = packed.at[peer * per_chip + j, halves]
                target, arrived = field.at[slot, me, half, halves], recv_sem.at[slot, me, half, part]

                def away():
                    copy = pltpu.make_async_remote_copy(
                        source, target, send_sem.at[j, part, far + levels - 1, x], arrived,
                        device_id={"wk": peer, "ar": core}, device_id_type=MESH,
                    )
                    copy.start() if starting else copy.wait_send()

                def here():
                    pltpu.make_async_copy(source, target, arrived).start()

                if far == 0:
                    mine = column * areas + half == x * areas + core
                    pl.when(jnp.logical_not(mine))(away)
                    if starting:
                        pl.when(mine)(here)
                else:
                    away()

        where_level(far, across)

    def both_ways(far):
        return (far, -far) if far else (0,)

    for far in range(levels):
        if far >= 2:
            learn(far)
            if far < levels - 1:
                pass_on(far)
        for way in both_ways(far):
            scatter(0, 0, way, True)
    for copy in to_twin:
        copy.start()
    far_first = [way for far in range(levels - 1, -1, -1) for way in both_ways(far)]
    for way in far_first:
        scatter(0, 1, way, True)
    for way in far_first:
        scatter(0, 2, way, True)
    for j in range(1, per_chip):
        for peer in range(peers):
            pack(peer * per_chip + j)
        for part in range(3):
            for way in far_first:
                scatter(j, part, way, True)

    def spread(block_row):
        for slot in range(slot_total):
            live = slot < count_all[block_row // rows_here, lax.rem(block_row, rows_here)]
            block = jnp.where(live, matrix[block_row, slot], 0.0)
            high = block.astype(jnp.bfloat16)
            low = (block - high.astype(jnp.float32)).astype(jnp.bfloat16)
            wide[block_row, slot * width : (slot + 1) * width, 0:width] = high
            wide[block_row, slot * width : (slot + 1) * width, width : 2 * width] = low

    own_matrix.wait()
    own_index.wait()
    own_count.wait()

    @pl.loop(0, rows_here)
    def _(n):
        spread(half * rows_here + n)

    for copy in to_twin:
        copy.wait_recv()

    @pl.loop(0, rows_here)
    def _(n):
        spread((1 - half) * rows_here + n)

    def prior(first_lag, second_lag):
        for a in range(areas):
            part = [direction[pl.ds(t * rows + a * rows_here, rows_here), :] for t in range(weeks)]
            inner = []
            for t in range(weeks):
                value = part[t]
                if t >= 1:
                    value = value - first_lag * part[t - 1]
                if t >= 2:
                    value = value - second_lag * part[t - 2]
                inner.append(value)
            for t in range(weeks):
                value = inner[t]
                if t + 1 < weeks:
                    value = value - first_lag * inner[t + 1]
                if t + 2 < weeks:
                    value = value - second_lag * inner[t + 2]
                temporal_rows[pl.ds(t * rows + a * rows_here, rows_here), :] = value
        for g in range(rows):
            value = temporal_rows[pl.ds(g, weeks, stride=rows), :]
            high = value.astype(jnp.bfloat16)
            operand[g, 0:weeks] = high
            operand[g, weeks : 2 * weeks] = (value - high.astype(jnp.float32)).astype(jnp.bfloat16)
        for n in range(rows):
            a, b = n // rows_here, n % rows_here
            left = jnp.concatenate([operand[index_all[a, s, b]] for s in range(slot_total)], axis=1)
            both = jnp.dot(left, wide[n], preferred_element_type=jnp.float32)
            value = both[0:weeks, 0:width] + (both[0:weeks, width:] + both[weeks:, 0:width])
            product[pl.ds(n, weeks, stride=rows), :] = value

    def total(values):
        return jnp.sum(values, axis=(0, 1), keepdims=True)

    def give(slot, far, starting):
        site = me * per_chip + half * site_slots + slot
        target, arrived = returned.at[site], return_sem.at[site]

        def across():
            for x in range(2):
                for a in range(areas):
                    peer = (level + far) * 2 + x
                    source = outgoing.at[slot, peer, a]

                    def away():
                        copy = pltpu.make_async_remote_copy(
                            source, target, back_sem.at[slot, far + levels - 1, x, a], arrived,
                            device_id={"wk": peer, "ar": a}, device_id_type=MESH,
                        )
                        copy.start() if starting else copy.wait_send()

                    def here():
                        pltpu.make_async_copy(source, target, arrived).start()

                    if far == 0:
                        mine = column * areas + half == x * areas + a
                        pl.when(jnp.logical_not(mine))(away)
                        if starting:
                            pl.when(mine)(here)
                    else:
                        away()

        where_level(far, across)

    def take(slot, part):
        halves = pl.ds(part, 1)
        for w in range(peers):
            for a in range(areas):
                pltpu.make_async_copy(
                    packed.at[0, halves], field.at[slot, w, a, halves], recv_sem.at[slot, w, a, part]
                ).wait()

    def unpack(slot, number, target):
        for w in range(peers):
            for a in range(areas):
                for t in range(weeks_here):
                    row = pl.ds((w * weeks_here + t) * rows + a * rows_here, rows_here)
                    target[row, :] = field[slot, w, a, number, t]

    @pl.loop(0, sites_here)
    def _(slot):
        site = me * per_chip + half * site_slots + slot
        scale, first_lag, second_lag = tau[site], phi_one[site], phi_two[site]
        take(slot, 0)
        unpack(slot, 0, direction)
        prior(first_lag, second_lag)
        take(slot, 1)
        unpack(slot, 1, residual)
        gradient = residual[...] - scale * product[...]
        residual[...] = gradient
        direction[...] = gradient
        search[...] = jnp.zeros_like(gradient)
        prior(first_lag, second_lag)
        take(slot, 2)
        unpack(slot, 2, mean)

        def step_length(norm_now):
            image = scale * product[...] + mean[...] * direction[...]
            return image, norm_now / total(direction[...] * image)

        def iteration(_, norm_now):
            image, alpha = step_length(norm_now)
            search[...] += alpha * direction[...]
            after = residual[...] - alpha * image
            residual[...] = after
            norm_next = total(after * after)
            direction[...] = after + (norm_next / norm_now) * direction[...]
            prior(first_lag, second_lag)
            return norm_next

        norm_last = lax.fori_loop(0, ITERS - 1, iteration, total(gradient * gradient))
        _, alpha = step_length(norm_last)
        search[...] += alpha * direction[...]
        for w in range(peers):
            for a in range(areas):
                for t in range(weeks_here):
                    row = pl.ds((w * weeks_here + t) * rows + a * rows_here, rows_here)
                    outgoing[slot, w, a, t] = search[row, :]
        for way in far_first:
            give(slot, way, True)

    for j in range(per_chip):
        for w in range(peers):
            site = w * per_chip + j
            pltpu.make_async_copy(outgoing.at[0, 0, 0], returned.at[site], return_sem.at[site]).wait()
            for week in range(weeks_here):
                row = pl.ds(site * rows_here * weeks_here + week, rows_here, stride=weeks_here)
                out[row, :] = latent[row, :] + returned[site, week]

    for copy in to_twin:
        copy.wait_send()
    for j in range(per_chip):
        for part in range(3):
            for way in far_first:
                scatter(j, part, way, False)

    @pl.loop(0, sites_here)
    def _(slot):
        for way in far_first:
            give(slot, way, False)


def by_site(
    peers, areas, latent, log_offset, case_counts, tau, phi_one, phi_two, blocks, block_index, block_count
):
    cancers, weeks_here, areas_here = latent.shape
    rows_here, slot_total, width, _ = blocks.shape
    if cancers % peers or peers % 2 or areas != 2 or rows_here % 8 or (peers * weeks_here) % 16:
        return local(latent, log_offset, case_counts, tau, phi_one, phi_two, blocks, block_index, block_count)
    per_chip = cancers // peers
    site_slots = -(-per_chip // areas)
    weeks, rows = peers * weeks_here, areas * rows_here

    def as_rows(value):
        split = value.reshape(cancers, weeks_here, rows_here, width)
        return split.transpose(0, 2, 1, 3).reshape(cancers * rows_here * weeks_here, width)

    f32, bf16 = jnp.float32, jnp.bfloat16
    tile = (weeks_here, rows_here, width)
    plane = pltpu.VMEM((weeks * rows, width), f32)
    dma = pltpu.SemaphoreType.DMA
    flat = (cancers * rows_here * weeks_here, width)
    scalars = pltpu.SMEM((cancers,), f32)
    operands = (
        as_rows(latent), as_rows(log_offset), as_rows(case_counts), tau, phi_one, phi_two,
        blocks, block_index.T, block_count,
    )
    result = pl.pallas_call(
        functools.partial(site_kernel, peers, areas, per_chip, weeks_here, rows_here, slot_total),
        out_shape=pltpu.VMEM(flat, f32),
        in_specs=[pl.BlockSpec(memory_space=pltpu.HBM)] * 9,
        out_specs=pl.BlockSpec(memory_space=pltpu.VMEM),
        scratch_shapes=[
            pltpu.VMEM(flat, f32), pltpu.VMEM(flat, f32), pltpu.VMEM(flat, jnp.int32), scalars, scalars, scalars,
            pltpu.VMEM((cancers, 3) + tile, f32),
            pltpu.VMEM((site_slots, peers, areas, 3) + tile, f32),
            pltpu.VMEM((rows, slot_total, width, width), f32),
            pltpu.VMEM((rows, slot_total * width, 2 * width), bf16),
            pltpu.SMEM((areas, slot_total, rows_here), jnp.int32),
            pltpu.SMEM((areas, rows_here), jnp.int32),
            plane,
            pltpu.VMEM((rows, 2 * weeks, width), bf16),
            plane, plane, plane, plane, plane,
            pltpu.VMEM((site_slots, peers, areas) + tile, f32),
            pltpu.VMEM((cancers,) + tile, f32),
            dma((6,)),
            dma((per_chip, 3, peers - 1, 2)),
            dma((site_slots, peers, areas, 3)),
            dma((3,)),
            dma((6,)),
            dma((site_slots, peers - 1, 2, areas)),
            dma((cancers,)),
            pltpu.SemaphoreType.REGULAR((2, peers // 2)),
        ],
        compiler_params=pltpu.CompilerParams(
            collective_id=0, has_side_effects=True, vmem_limit_bytes=40 * 1024 * 1024
        ),
    )(*(pltpu.with_memory_space_constraint(operand, pltpu.HBM) for operand in operands))
    split = result.reshape(cancers, rows_here, weeks_here, width).transpose(0, 2, 1, 3)
    return split.reshape(latent.shape)


def solution(mesh):
    return jax.shard_map(
        functools.partial(by_site, mesh.shape["wk"], mesh.shape["ar"]),
        mesh=mesh,
        in_specs=(
            P("grp", "wk", "ar"),
            P("grp", "wk", "ar"),
            P("grp", "wk", "ar"),
            P(),
            P(),
            P(),
            P("ar", None, None, None),
            P("ar", None),
            P("ar"),
        ),
        out_specs=P("grp", "wk", "ar"),
        check_vma=False,
    )
```
